32 devices in a mesh: lat: 4 (over x, core), lon: 8 (over z, y).
Axes of the slice: x: 2, y: 2, z: 4, core: 2. Of those that a mesh axis runs over, the one named last changes fastest.
Arguments:
- tendencies: bfloat16 [3, 64, 2880, 128], P(None, 'lat', 'lon'), may hold values from -6 to 6
- bands: int32 [64], replicated, may hold values from 45 to 180
- winds: float32 [2, 64, 2880, 128], P(None, 'lat', 'lon'), may hold values from -6 to 6
- tracers: float32 [5, 64, 2880, 128], P(None, 'lat', 'lon'), may hold values from -6 to 6
Outputs:
- filtered: bfloat16 [3, 64, 2880, 128], P(None, 'lat', 'lon')
- advected: float32 [5, 64, 2880, 128], P(None, 'lat', 'lon')
The draws below stay inside these ranges and needn't reach their ends.
All inputs are finite; a program needn't handle non-finite values.
Results may differ from the reference program's by a relative error of at most 0.0038.
Values may be sent and summed in bfloat16 or wider, within the bound.
A program may use at most 192 MiB of HBM per device.

```python
import jax
import jax.numpy as jnp
from jax import lax

NLON = 2880
HEMI = 720
LEV = 128
FIELDS = 3
TRACERS = 5
NLAT = 64
J0 = 328


def plant(array, own_key, smallest, high):
    longest = array.shape.index(max(array.shape))
    spots = []
    for shift in (0, 1):
        where = [jax.random.randint(jax.random.fold_in(own_key, axis), (), 0, length) for axis, length in enumerate(array.shape)]
        where[longest] = (where[longest] + shift) % array.shape[longest]
        spots.append(tuple(where))
    return array.at[spots[0]].set(smallest).at[spots[1]].set(high)


def level_of(rng, dims, split, low, high):
    level, own = 1.0, jax.random.fold_in(rng, 6)
    for dim, shards_of in split:
        draws = jnp.exp(jax.random.uniform(jax.random.fold_in(own, dim), (shards_of,), jnp.float32, low / len(split), high / len(split)))
        level = level * jnp.repeat(draws, dims[dim] // shards_of).reshape([-1 if axis == dim else 1 for axis in range(len(dims))])
    return level


def bell_draw(own_key, dims, scale, reach, cuts=(), held_as=jnp.bfloat16):
    drawn = jax.random.normal(own_key, dims, jnp.float32) * scale
    if len(cuts) > 0:
        drawn = level_of(own_key, dims, cuts, -0.22, 0.18) * drawn
    return jnp.clip(drawn, min=-reach, max=reach).astype(held_as)


def setup_inputs(seed: int = 0) -> dict:
    arg_keys = jax.random.split(jax.random.key(seed), 5)
    return {
        "tendencies": bell_draw(arg_keys[0], (FIELDS, NLAT, NLON, LEV), 1.0, 6.0, ((1, 4), (2, 8))),
        "bands": plant(jax.random.randint(arg_keys[1], (NLAT,), NLON // 64, NLON // 16 + 1), jax.random.fold_in(arg_keys[1], 1), NLON // 64, (NLON // 16 + 1) - 1).astype(jnp.int32),
        "winds": bell_draw(arg_keys[2], (2, NLAT, NLON, LEV), 1.0, 6.0, ((1, 4), (2, 8)), jnp.float32),
        "tracers": bell_draw(arg_keys[3], (TRACERS, NLAT, NLON, LEV), 1.0, 6.0, ((1, 4), (2, 8)), jnp.float32),
    }


def reference(tendencies, bands, winds, tracers):
    lat_count = tendencies.shape[1]
    lon_count = tendencies.shape[2]
    half_wave = lon_count // 2
    row_index = jnp.arange(lat_count, dtype=jnp.float32)
    grid_row = row_index + jnp.float32(J0)
    centre_cos = jnp.sin(jnp.pi * (grid_row + 0.5) / (2.0 * HEMI))
    face_cos = jnp.sin(jnp.pi * grid_row / (2.0 * HEMI))
    damping = 0.25 + 0.5 * (row_index + 0.5) / (lat_count / 2.0)
    wave_index = jnp.arange(half_wave + 1, dtype=jnp.int32)
    polar_rows = jnp.arange(lat_count, dtype=jnp.int32) < lat_count // 2
    retained = (wave_index[None, :] <= bands[:, None]) | jnp.logical_not(polar_rows[:, None])
    multiplier = jnp.where(retained, jnp.float32(1.0), damping[:, None]).astype(jnp.float32)

    def filter_field(one_field):
        spectrum = jnp.fft.rfft(one_field.astype(jnp.float32), axis=1)
        return jnp.fft.irfft(spectrum * multiplier[:, :, None], n=lon_count, axis=1).astype(jnp.float32)

    filtered = lax.map(filter_field, tendencies).astype(jnp.bfloat16)
    new_winds = winds + filtered[0:2].astype(jnp.float32)
    east_courant = 0.5 * jnp.tanh(new_winds[0])
    north_courant = 0.25 * jnp.tanh(new_winds[1])
    west_cells = jnp.roll(tracers, 1, axis=2)
    f_west = jnp.maximum(east_courant, 0.0) * west_cells + jnp.minimum(east_courant, 0.0) * tracers
    f_east = jnp.roll(f_west, -1, axis=2)
    prior_rows = jnp.concatenate([jnp.zeros_like(tracers[:, :1]), tracers[:, :-1]], axis=1)
    g_pole = face_cos[:, None, None] * (jnp.maximum(north_courant, 0.0) * prior_rows + jnp.minimum(north_courant, 0.0) * tracers)
    g_next = jnp.concatenate([g_pole[:, 1:], jnp.zeros_like(g_pole[:, :1])], axis=1)
    advected = tracers - (f_east - f_west) - (g_next - g_pole) / centre_cos[:, None, None]
    return filtered, advected
```

```python
import functools
import math

import jax
import jax.numpy as jnp
import numpy as np
from jax import lax
from jax.experimental import pallas as pl
from jax.experimental.pallas import tpu as pltpu
from jax.sharding import PartitionSpec as P

HEMI = 720
CHUNK = 24
VMEM_BYTES = 48 * 1024 * 1024
FACTOR_FLOOR = 1e-7


def latitude_factors(row_ids, lat_count):
    grid_row = row_ids.astype(jnp.float32) + jnp.float32(HEMI // 2 - lat_count // 2)
    centre_cos = jnp.sin(math.pi * (grid_row + 0.5) / (2.0 * HEMI))
    face_cos = jnp.sin(math.pi * grid_row / (2.0 * HEMI))
    return (centre_cos, face_cos)


@functools.lru_cache(maxsize=None)
def cosecant_factors(lon_count, width):
    cells = np.arange(width)
    apart = cells[:, None] - cells[None, :]
    safe = np.where(apart == 0, 1, apart)
    own = np.where(apart == 0, 0.0, 1.0 / (lon_count * np.sin(np.pi * safe / lon_count)))
    targets, sources, shifts = [], [], []
    for shift in range(1, lon_count // width):
        block = 1.0 / (lon_count * np.sin(np.pi * (apart + shift * width) / lon_count))
        left, values, right = np.linalg.svd(block)
        rank = max(4, -4 * (-int((values > FACTOR_FLOOR).sum()) // 4))
        root = np.sqrt(values[:rank])
        targets.append(np.tile(left[:, :rank] * root, (1, 2)))
        sources.append(np.tile(root[:, None] * right[:rank], (2, 1)))
        shifts.append((shift, rank))
    return own, np.concatenate(targets, 1), np.concatenate(sources, 0), tuple(shifts)


def filter_tables(odd, strength, lon_count, width):
    own, targets, sources, shifts = cosecant_factors(lon_count, width)

    def phase(cells):
        return (odd[:, None] * cells[None, :] % (2 * lon_count)).astype(jnp.float32) * (
            math.pi / lon_count
        )

    here = phase(jnp.arange(width, dtype=jnp.int32))
    sin_here, cos_here = jnp.sin(here), jnp.cos(here)
    near = (
        sin_here[:, :, None] * cos_here[:, None, :] - cos_here[:, :, None] * sin_here[:, None, :]
    ) * jnp.asarray(own, jnp.float32)
    near = near + jnp.eye(width, dtype=jnp.float32) * (odd.astype(jnp.float32) / lon_count)[
        :, None, None
    ]
    near = (near * strength[:, None, None]).astype(jnp.bfloat16)
    offsets = np.concatenate([np.full(2 * rank, shift * width) for shift, rank in shifts])
    is_sin = np.concatenate([np.repeat([False, True], rank) for _, rank in shifts])
    moved = phase(jnp.asarray(offsets, jnp.int32)) - jnp.asarray(
        np.where(is_sin, math.pi / 2, 0.0), jnp.float32
    )
    far = sin_here[:, :, None] * jnp.cos(moved)[:, None, :] + cos_here[:, :, None] * jnp.sin(moved)[
        :, None, :
    ]
    far = (far * jnp.asarray(targets, jnp.float32) * strength[:, None, None]).astype(jnp.bfloat16)
    send = jnp.where(is_sin[None, :, None], sin_here[:, None, :], cos_here[:, None, :])
    send = (send * jnp.asarray(sources, jnp.float32)).astype(jnp.bfloat16)
    return near, far, send, shifts


def project_kernel(x_ref, send_ref, out_ref):
    row = jnp.concatenate([x_ref[f, 0] for f in range(x_ref.shape[0])], axis=1)
    out_ref[0] = jnp.dot(send_ref[0], row, preferred_element_type=jnp.float32).astype(out_ref.dtype)


def project(tendencies, send):
    fields, rows, width, lev = tendencies.shape
    count = send.shape[1]
    return pl.pallas_call(
        project_kernel,
        grid=(rows,),
        in_specs=[
            pl.BlockSpec((fields, 1, width, lev), lambda j: (0, j, 0, 0)),
            pl.BlockSpec((1, count, width), lambda j: (j, 0, 0)),
        ],
        out_specs=pl.BlockSpec((1, count, fields * lev), lambda j: (j, 0, 0)),
        out_shape=jax.ShapeDtypeStruct((rows, count, fields * lev), jnp.bfloat16),
        compiler_params=pltpu.CompilerParams(vmem_limit_bytes=VMEM_BYTES),
        cost_estimate=pl.CostEstimate(
            flops=2 * rows * count * width * fields * lev,
            bytes_accessed=2 * tendencies.size + 2 * send.size,
            transcendentals=0,
        ),
        name="project_tendencies",
    )(tendencies, send)


def filter_kernel(keep_ref, x_ref, near_ref, far_ref, coef_ref, winds_ref, filtered_ref, courant_ref):
    fields, _, _, lev = x_ref.shape
    keep = keep_ref[pl.program_id(0)]
    row = jnp.concatenate([x_ref[f, 0] for f in range(fields)], axis=1)
    total = jnp.dot(near_ref[0], row, preferred_element_type=jnp.float32)
    total = total + jnp.dot(far_ref[0], coef_ref[0], preferred_element_type=jnp.float32)
    for f in range(fields):
        value = keep * x_ref[f, 0].astype(jnp.float32) + total[:, f * lev : (f + 1) * lev]
        value = value.astype(jnp.bfloat16)
        filtered_ref[f, 0] = value
        if f < 2:
            wind = winds_ref[f, 0] + value.astype(jnp.float32)
            courant_ref[f, 0] = (0.5 if f == 0 else 0.25) * jnp.tanh(wind)


def filter_rows(keep, tendencies, near, far, coefs, winds):
    fields, rows, width, lev = tendencies.shape
    count = far.shape[2]
    return pl.pallas_call(
        filter_kernel,
        grid=(rows,),
        in_specs=[
            pl.BlockSpec(memory_space=pltpu.SMEM),
            pl.BlockSpec((fields, 1, width, lev), lambda j: (0, j, 0, 0)),
            pl.BlockSpec((1, width, width), lambda j: (j, 0, 0)),
            pl.BlockSpec((1, width, count), lambda j: (j, 0, 0)),
            pl.BlockSpec((1, count, fields * lev), lambda j: (j, 0, 0)),
            pl.BlockSpec((2, 1, width, lev), lambda j: (0, j, 0, 0)),
        ],
        out_specs=[
            pl.BlockSpec((fields, 1, width, lev), lambda j: (0, j, 0, 0)),
            pl.BlockSpec((2, 1, width, lev), lambda j: (0, j, 0, 0)),
        ],
        out_shape=[
            jax.ShapeDtypeStruct(tendencies.shape, jnp.bfloat16),
            jax.ShapeDtypeStruct(winds.shape, jnp.float32),
        ],
        compiler_params=pltpu.CompilerParams(vmem_limit_bytes=VMEM_BYTES),
        cost_estimate=pl.CostEstimate(
            flops=2 * rows * (width + count) * width * fields * lev,
            bytes_accessed=4 * tendencies.size + 8 * winds.size,
            transcendentals=winds.size,
        ),
        name="filter_rows",
    )(keep, tendencies, near, far, coefs, winds)


def advect_kernel(
    face_ref, inverse_ref, tracer_ref, courant_ref, prior_ref, next_ref, west_ref, east_ref,
    north_ref, zonal_ref, out_ref, before, partial, edge, shifted,
):
    tracers, _, width, _ = tracer_ref.shape
    step = pl.program_id(0)
    rows = pl.num_programs(0) - 1
    face = face_ref[step]
    inverse_before = inverse_ref[jnp.maximum(step - 1, 0)]
    chunks = [(start, min(CHUNK, width - start)) for start in range(0, width, CHUNK)]

    @pl.when(step == 0)
    def _():
        before[...] = prior_ref[:, 0]
        partial[...] = jnp.zeros_like(partial)

    @pl.when(step < rows)
    def _():
        inverse = inverse_ref[jnp.minimum(step, rows - 1)]
        shifted[0:width, :] = courant_ref[0, 0]
        shifted[width : width + 1, :] = zonal_ref[0]
        for start, size in chunks:
            part = pl.ds(start, size)
            here = courant_ref[0, 0, part, :]
            there = shifted[pl.ds(start + 1, size), :]
            north = courant_ref[1, 0, part, :]
            here_up, here_down = jnp.maximum(here, 0.0), jnp.minimum(here, 0.0)
            there_up, there_down = jnp.maximum(there, 0.0), jnp.minimum(there, 0.0)
            north_up = face * jnp.maximum(north, 0.0)
            north_down = face * jnp.minimum(north, 0.0)
            for q in range(tracers):
                value = tracer_ref[q, 0, part, :]
                if start == 0:
                    edge[q, 7:8, :] = west_ref[q, 0]
                    edge[q, pl.ds(8, size), :] = value
                    west = edge[q, pl.ds(7, size), :]
                else:
                    west = tracer_ref[q, 0, pl.ds(start - 1, size), :]
                if start + size == width:
                    edge[q, pl.ds(8, size), :] = value
                    edge[q, pl.ds(8 + size, 1), :] = east_ref[q, 0]
                    east = edge[q, pl.ds(9, size), :]
                else:
                    east = tracer_ref[q, 0, pl.ds(start + 1, size), :]
                flux = north_up * before[q, part, :] + north_down * value
                out_ref[q, 0, part, :] = partial[q, part, :] - flux * inverse_before
                zonal = (there_up * value + there_down * east) - (here_up * west + here_down * value)
                partial[q, part, :] = value - zonal + flux * inverse
                before[q, part, :] = value

    @pl.when(step == rows)
    def _():
        for start, size in chunks:
            part = pl.ds(start, size)
            north = north_ref[part, :]
            north_up = face * jnp.maximum(north, 0.0)
            north_down = face * jnp.minimum(north, 0.0)
            for q in range(tracers):
                flux = north_up * before[q, part, :] + north_down * next_ref[q, 0, part, :]
                out_ref[q, 0, part, :] = partial[q, part, :] - flux * inverse_before


def advect(face, inverse, tracers, courants, prior, following, west, east, north, zonal):
    count, rows, width, lev = tracers.shape

    def clipped(j):
        return jnp.minimum(j, rows - 1)

    row_halo = pl.BlockSpec((count, 1, width, lev), lambda j: (0, 0, 0, 0))
    column_halo = pl.BlockSpec((count, 1, 1, lev), lambda j: (0, clipped(j), 0, 0))
    return pl.pallas_call(
        advect_kernel,
        grid=(rows + 1,),
        in_specs=[
            pl.BlockSpec(memory_space=pltpu.SMEM),
            pl.BlockSpec(memory_space=pltpu.SMEM),
            pl.BlockSpec((count, 1, width, lev), lambda j: (0, clipped(j), 0, 0)),
            pl.BlockSpec((2, 1, width, lev), lambda j: (0, clipped(j), 0, 0)),
            row_halo,
            row_halo,
            column_halo,
            column_halo,
            pl.BlockSpec((width, lev), lambda j: (0, 0)),
            pl.BlockSpec((1, 1, lev), lambda j: (clipped(j), 0, 0)),
        ],
        out_specs=pl.BlockSpec((count, 1, width, lev), lambda j: (0, jnp.maximum(j - 1, 0), 0, 0)),
        out_shape=jax.ShapeDtypeStruct(tracers.shape, jnp.float32),
        scratch_shapes=[
            pltpu.VMEM((count, width, lev), jnp.float32),
            pltpu.VMEM((count, width, lev), jnp.float32),
            pltpu.VMEM((count, CHUNK + 16, lev), jnp.float32),
            pltpu.VMEM((width + 8, lev), jnp.float32),
        ],
        compiler_params=pltpu.CompilerParams(vmem_limit_bytes=VMEM_BYTES),
        cost_estimate=pl.CostEstimate(
            flops=20 * tracers.size, bytes_accessed=8 * tracers.size, transcendentals=0
        ),
        name="advect_rows",
    )(face, inverse, tracers, courants, prior, following, west, east, north, zonal)


def per_device(tendencies, bands, winds, tracers):
    lat_rows, width = tendencies.shape[1:3]
    lat_devices, lon_devices = lax.axis_size("lat"), lax.axis_size("lon")
    lat_count, lon_count = lat_devices * lat_rows, lon_devices * width
    half = lat_count // 2

    lat_on = [(i, i + 1) for i in range(lat_devices - 1)]
    lat_back = [(i + 1, i) for i in range(lat_devices - 1)]
    lon_on = [(i, (i + 1) % lon_devices) for i in range(lon_devices)]
    lon_back = [((i + 1) % lon_devices, i) for i in range(lon_devices)]

    def passed(block, axis, pairs):
        return lax.ppermute(block.astype(jnp.bfloat16), axis, pairs).astype(jnp.float32)

    own_ids = lax.axis_index("lat") * lat_rows + jnp.arange(lat_rows, dtype=jnp.int32)
    damping = 0.25 + 0.5 * (own_ids.astype(jnp.float32) + 0.5) / (lat_count / 2.0)
    keep = jnp.where(own_ids < half, damping, 1.0)
    near, far, send, shifts = filter_tables(
        2 * jnp.take(bands, own_ids) + 1, 1.0 - keep, lon_count, width
    )

    sent = project(tendencies, send)
    received, offset = [], 0
    for shift, rank in shifts:
        pairs = [
            (lat * lon_devices + i, lat * lon_devices + (i + shift) % lon_devices)
            for lat in range(lat_devices)
            if lat * lat_rows < half
            for i in range(lon_devices)
        ]
        piece = sent[:, offset : offset + 2 * rank]
        received.append(lax.ppermute(piece, ("lat", "lon"), pairs))
        offset += 2 * rank

    prior = passed(tracers[:, -1:], "lat", lat_on)
    following = passed(tracers[:, :1], "lat", lat_back)
    west = passed(tracers[:, :, -1:], "lon", lon_on)
    east = passed(tracers[:, :, :1], "lon", lon_back)

    filtered, courants = filter_rows(
        keep, tendencies, near, far, jnp.concatenate(received, axis=1), winds
    )
    north = passed(courants[1, 0], "lat", lat_back)
    zonal = passed(courants[0, :, :1], "lon", lon_back)

    centre_cos, _ = latitude_factors(own_ids, lat_count)
    first = lax.axis_index("lat") * lat_rows
    _, face_cos = latitude_factors(
        first + jnp.arange(lat_rows + 1, dtype=jnp.int32), lat_count
    )
    advected = advect(
        face_cos, 1.0 / centre_cos, tracers, courants, prior, following, west, east, north, zonal
    )
    return (filtered, advected)


def solution(mesh):
    spec = P(None, "lat", "lon", None)
    return jax.shard_map(
        per_device,
        mesh=mesh,
        in_specs=(spec, P(), spec, spec),
        out_specs=(spec, spec),
        check_vma=False,
    )
```

```python
import functools
import math

import jax
import jax.numpy as jnp
import numpy as np
from jax import lax
from jax.experimental import pallas as pl
from jax.experimental.pallas import tpu as pltpu
from jax.sharding import PartitionSpec as P

HEMI = 720
CHUNK = 24
VMEM_BYTES = 56 * 1024 * 1024
FACTOR_FLOOR = 1e-7


def latitude_factors(row_ids, lat_count):
    grid_row = row_ids.astype(jnp.float32) + jnp.float32(HEMI // 2 - lat_count // 2)
    centre_cos = jnp.sin(math.pi * (grid_row + 0.5) / (2.0 * HEMI))
    face_cos = jnp.sin(math.pi * grid_row / (2.0 * HEMI))
    return (centre_cos, face_cos)


@functools.lru_cache(maxsize=None)
def cosecant_factors(lon_count, width, group):
    cells = np.arange(width)
    apart = cells[:, None] - cells[None, :]
    safe = np.where(apart == 0, 1, apart)
    own = np.where(apart == 0, 0.0, 1.0 / (lon_count * np.sin(np.pi * safe / lon_count)))
    step = 8 // group
    targets, sources, offsets, is_sin, member, spans = [], [], [], [], [], []
    start = 0
    for shift in range(1, lon_count // width):
        block = 1.0 / (lon_count * np.sin(np.pi * (apart + shift * width) / lon_count))
        left, values, right = np.linalg.svd(block)
        rank = max(step, -(-int((values > FACTOR_FLOOR).sum()) // step) * step)
        root = np.sqrt(values[:rank])
        targets.append(np.tile(left[:, :rank] * root, (1, 2 * group)))
        sources.append(np.tile(root[:, None] * right[:rank], (2 * group, 1)))
        offsets.append(np.full(2 * group * rank, shift * width))
        is_sin.append(np.tile(np.repeat([False, True], rank), group))
        member.append(np.repeat(np.arange(group), 2 * rank))
        spans.append((shift, start, 2 * group * rank))
        start += 2 * group * rank
    return (
        own,
        np.concatenate(targets, 1),
        np.concatenate(sources, 0),
        np.concatenate(offsets),
        np.concatenate(is_sin),
        np.concatenate(member),
        tuple(spans),
    )


def filter_tables(odd, strength, lon_count, width, group):
    own, targets, sources, offsets, is_sin, member, spans = cosecant_factors(
        lon_count, width, group
    )

    def phase(cells):
        return (odd[:, None] * cells[None, :] % (2 * lon_count)).astype(jnp.float32) * (
            math.pi / lon_count
        )

    here = phase(jnp.arange(width, dtype=jnp.int32))
    sin_here, cos_here = jnp.sin(here), jnp.cos(here)
    near = (
        sin_here[:, :, None] * cos_here[:, None, :] - cos_here[:, :, None] * sin_here[:, None, :]
    ) * jnp.asarray(own, jnp.float32)
    near = near + jnp.eye(width, dtype=jnp.float32) * (odd.astype(jnp.float32) / lon_count)[
        :, None, None
    ]
    near = (near * strength[:, None, None]).astype(jnp.bfloat16)
    own_column = member[None, :] == np.arange(odd.shape[0])[:, None] % group
    moved = phase(jnp.asarray(offsets, jnp.int32)) - jnp.asarray(
        np.where(is_sin, math.pi / 2, 0.0), jnp.float32
    )
    weight = strength[:, None] * own_column
    far = (
        sin_here[:, :, None] * (weight * jnp.cos(moved))[:, None, :]
        + cos_here[:, :, None] * (weight * jnp.sin(moved))[:, None, :]
    )
    far = (far * jnp.asarray(targets, jnp.float32)).astype(jnp.bfloat16)
    use_sin = (own_column & is_sin).astype(np.float32)
    use_cos = (own_column & ~is_sin).astype(np.float32)
    send = use_sin[:, :, None] * sin_here[:, None, :] + use_cos[:, :, None] * cos_here[:, None, :]
    send = (send * jnp.asarray(sources, jnp.float32)).astype(jnp.bfloat16)
    return near, far, send, spans


def filter_kernel(
    spans, group, keep_ref, x_ref, send_ref, near_ref, far_ref, winds_ref, tracers_ref,
    filtered_ref, courant_ref, prior_ref, next_ref, west_ref, east_ref, north_ref, zonal_ref,
    winds, filtered, courants, total, outgoing, incoming, low_block, high_block, low, high, column,
    local_sem, send_sem, recv_sem, halo_send, halo_recv,
):
    fields, rows, width, lev = x_ref.shape
    tracer_count = tracers_ref.shape[0]
    lat, lon = lax.axis_index("lat"), lax.axis_index("lon")
    lat_devices, lon_devices = lax.axis_size("lat"), lax.axis_size("lon")
    has_prior, has_next = lat > 0, lat < lat_devices - 1
    lat_prior, lat_next = jnp.maximum(lat - 1, 0), jnp.minimum(lat + 1, lat_devices - 1)
    lon_west, lon_east = lax.rem(lon + lon_devices - 1, lon_devices), lax.rem(lon + 1, lon_devices)
    last_start = (width - 1) // 8 * 8

    winds_copy = pltpu.make_async_copy(winds_ref, winds, local_sem.at[0])
    low_copy = pltpu.make_async_copy(tracers_ref.at[:, :, pl.ds(0, 8)], low_block, local_sem.at[1])
    high_copy = pltpu.make_async_copy(
        tracers_ref.at[:, :, pl.ds(last_start, width - last_start)], high_block, local_sem.at[2]
    )
    low_copy.start()
    high_copy.start()
    winds_copy.start()

    barrier = pltpu.get_barrier_semaphore()
    for shift in range(1, lon_devices):
        pl.semaphore_signal(
            barrier, inc=1, device_id=(lat, lax.rem(lon + shift, lon_devices)),
            device_id_type=pl.DeviceIdType.MESH,
        )

    @pl.when(has_prior)
    def _():
        pl.semaphore_signal(
            barrier, inc=1, device_id=(lat_prior, lon), device_id_type=pl.DeviceIdType.MESH
        )

    @pl.when(has_next)
    def _():
        pl.semaphore_signal(
            barrier, inc=1, device_id=(lat_next, lon), device_id_type=pl.DeviceIdType.MESH
        )

    def field_row(j):
        return jnp.concatenate([x_ref[f, j] for f in range(fields)], axis=1)

    def project(p, carry):
        parts = [
            jnp.dot(send_ref[p * group + g], field_row(p * group + g), preferred_element_type=jnp.float32)
            for g in range(group)
        ]
        outgoing[p] = sum(parts[1:], parts[0]).astype(jnp.bfloat16)
        return carry

    lax.fori_loop(0, rows // group, project, 0)
    pl.semaphore_wait(barrier, lon_devices - 1 + has_prior.astype(jnp.int32) + has_next.astype(jnp.int32))

    def remote(source, target, sems, slot, device):
        return pltpu.make_async_remote_copy(
            src_ref=source, dst_ref=target, send_sem=sems[0].at[slot], recv_sem=sems[1].at[slot],
            device_id=device, device_id_type=pl.DeviceIdType.MESH,
        )

    exchanges = []
    for slot, (shift, start, size) in enumerate(spans):
        part = pl.ds(start, size)
        exchanges.append(
            remote(
                outgoing.at[:, part], incoming.at[:, part], (send_sem, recv_sem), slot,
                (lat, lax.rem(lon + shift, lon_devices)),
            )
        )
    for exchange in exchanges:
        exchange.start()

    halo = (halo_send, halo_recv)
    to_next = remote(tracers_ref.at[:, rows - 1], prior_ref, halo, 0, (lat_next, lon))
    to_prior = remote(tracers_ref.at[:, 0], next_ref, halo, 1, (lat_prior, lon))
    to_east = remote(high, west_ref, halo, 2, (lat, lon_east))
    to_west = remote(low, east_ref, halo, 3, (lat, lon_west))
    north_to_prior = remote(courants.at[1, 0], north_ref, halo, 4, (lat_prior, lon))
    zonal_to_west = remote(column, zonal_ref, halo, 5, (lat, lon_west))

    @pl.when(has_next)
    def _():
        to_next.start()

    @pl.when(has_prior)
    def _():
        to_prior.start()

    low_copy.wait()
    high_copy.wait()
    for q in range(tracer_count):
        for j in range(rows):
            low[q, j : j + 1, :] = low_block[q, j, 0:1, :]
            high[q, j : j + 1, :] = high_block[q, j, width - 1 - last_start : width - last_start, :]
    to_east.start()
    to_west.start()

    def near_row(j, carry):
        total[j] = jnp.dot(near_ref[j], field_row(j), preferred_element_type=jnp.float32)
        return carry

    lax.fori_loop(0, rows, near_row, 0)
    winds_copy.wait()
    for exchange in exchanges:
        exchange.wait_recv()

    def outputs(j):
        return (
            pltpu.make_async_copy(filtered.at[:, j], filtered_ref.at[:, j], local_sem.at[3]),
            pltpu.make_async_copy(courants.at[:, j], courant_ref.at[:, j], local_sem.at[4]),
        )

    def finish(j):
        far = jnp.dot(far_ref[j], incoming[j // group], preferred_element_type=jnp.float32)
        for f in range(fields):
            lanes = slice(f * lev, (f + 1) * lev)
            value = keep_ref[j] * x_ref[f, j].astype(jnp.float32) + total[j, :, lanes] + far[:, lanes]
            value = value.astype(jnp.bfloat16)
            filtered[f, j] = value
            if f < 2:
                courant = (0.5 if f == 0 else 0.25) * jnp.tanh(winds[f, j] + value.astype(jnp.float32))
                courants[f, j] = courant
                if f == 0:
                    column[pl.ds(j, 1), :] = courant[0:1, :]
        for copy in outputs(j):
            copy.start()

    finish(0)

    @pl.when(has_prior)
    def _():
        north_to_prior.start()

    def later(j, carry):
        finish(j)
        return carry

    lax.fori_loop(1, rows, later, 0)
    zonal_to_west.start()

    for exchange in exchanges:
        exchange.wait_send()
    to_east.wait()
    to_west.wait()
    zonal_to_west.wait()

    @pl.when(has_next)
    def _():
        to_next.wait_send()
        to_prior.wait_recv()
        north_to_prior.wait_recv()

    @pl.when(has_prior)
    def _():
        to_next.wait_recv()
        to_prior.wait_send()
        north_to_prior.wait_send()

    pltpu.make_async_copy(filtered, filtered_ref, local_sem.at[3]).wait()
    pltpu.make_async_copy(courants, courant_ref, local_sem.at[4]).wait()


def filter_rows(keep, tendencies, send, near, far, winds, tracers, spans, group):
    fields, rows, width, lev = tendencies.shape
    count = far.shape[2]
    tracer_count = tracers.shape[0]
    last = width - (width - 1) // 8 * 8
    hbm = pl.BlockSpec(memory_space=pl.ANY)
    vmem = pl.BlockSpec(memory_space=pltpu.VMEM)
    f32 = jnp.float32
    exchanged = (rows // group, count, fields * lev)
    return pl.pallas_call(
        functools.partial(filter_kernel, spans, group),
        in_specs=[pl.BlockSpec(memory_space=pltpu.SMEM), vmem, vmem, vmem, vmem, hbm, hbm],
        out_specs=[hbm] * 8,
        out_shape=[
            jax.ShapeDtypeStruct(tendencies.shape, jnp.bfloat16),
            jax.ShapeDtypeStruct(winds.shape, f32),
            jax.ShapeDtypeStruct((tracer_count, width, lev), f32),
            jax.ShapeDtypeStruct((tracer_count, width, lev), f32),
            jax.ShapeDtypeStruct((tracer_count, rows, lev), f32),
            jax.ShapeDtypeStruct((tracer_count, rows, lev), f32),
            jax.ShapeDtypeStruct((width, lev), f32),
            jax.ShapeDtypeStruct((rows, lev), f32),
        ],
        scratch_shapes=[
            pltpu.VMEM(winds.shape, f32),
            pltpu.VMEM(tendencies.shape, jnp.bfloat16),
            pltpu.VMEM(winds.shape, f32),
            pltpu.VMEM((rows, width, fields * lev), f32),
            pltpu.VMEM(exchanged, jnp.bfloat16),
            pltpu.VMEM(exchanged, jnp.bfloat16),
            pltpu.VMEM((tracer_count, rows, 8, lev), f32),
            pltpu.VMEM((tracer_count, rows, last, lev), f32),
            pltpu.VMEM((tracer_count, rows, lev), f32),
            pltpu.VMEM((tracer_count, rows, lev), f32),
            pltpu.VMEM((rows, lev), f32),
            pltpu.SemaphoreType.DMA((5,)),
            pltpu.SemaphoreType.DMA((len(spans),)),
            pltpu.SemaphoreType.DMA((len(spans),)),
            pltpu.SemaphoreType.DMA((6,)),
            pltpu.SemaphoreType.DMA((6,)),
        ],
        compiler_params=pltpu.CompilerParams(
            vmem_limit_bytes=VMEM_BYTES, collective_id=0, has_side_effects=True
        ),
        cost_estimate=pl.CostEstimate(
            flops=2 * rows * (width + 2 * count) * width * fields * lev,
            bytes_accessed=4 * tendencies.size + 8 * winds.size,
            transcendentals=winds.size,
        ),
        name="filter_rows",
    )(keep, tendencies, send, near, far, winds, tracers)


def advect_kernel(
    edges_ref, face_ref, inverse_ref, tracer_ref, courant_ref, passing_ref, prior_ref, next_ref,
    west_ref, east_ref, north_ref, zonal_ref, out_ref, passed_ref, before, partial, edge, shifted,
):
    tracers, _, width, _ = tracer_ref.shape
    step = pl.program_id(0)
    rows = pl.num_programs(0) - 1
    face = face_ref[step]
    inverse_before = inverse_ref[jnp.maximum(step - 1, 0)]
    chunks = [(start, min(CHUNK, width - start)) for start in range(0, width, CHUNK)]

    @pl.when(step == 0)
    def _():
        before[...] = jnp.where(edges_ref[0] > 0, prior_ref[...], 0.0)
        partial[...] = jnp.zeros_like(partial)

    @pl.when(step < rows)
    def _():
        inverse = inverse_ref[jnp.minimum(step, rows - 1)]
        passed_ref[...] = passing_ref[...]
        shifted[0:width, :] = courant_ref[0, 0]
        shifted[width : width + 1, :] = zonal_ref[pl.ds(step, 1), :]
        for start, size in chunks:
            part = pl.ds(start, size)
            here = courant_ref[0, 0, part, :]
            there = shifted[pl.ds(start + 1, size), :]
            north = courant_ref[1, 0, part, :]
            here_up, here_down = jnp.maximum(here, 0.0), jnp.minimum(here, 0.0)
            there_up, there_down = jnp.maximum(there, 0.0), jnp.minimum(there, 0.0)
            north_up = face * jnp.maximum(north, 0.0)
            north_down = face * jnp.minimum(north, 0.0)
            for q in range(tracers):
                value = tracer_ref[q, 0, part, :]
                if start == 0:
                    edge[q, 7:8, :] = west_ref[q, pl.ds(step, 1), :]
                    edge[q, pl.ds(8, size), :] = value
                    west = edge[q, pl.ds(7, size), :]
                else:
                    west = tracer_ref[q, 0, pl.ds(start - 1, size), :]
                if start + size == width:
                    edge[q, pl.ds(8, size), :] = value
                    edge[q, pl.ds(8 + size, 1), :] = east_ref[q, pl.ds(step, 1), :]
                    east = edge[q, pl.ds(9, size), :]
                else:
                    east = tracer_ref[q, 0, pl.ds(start + 1, size), :]
                flux = north_up * before[q, part, :] + north_down * value
                out_ref[q, 0, part, :] = partial[q, part, :] - flux * inverse_before
                zonal = (there_up * value + there_down * east) - (here_up * west + here_down * value)
                partial[q, part, :] = value - zonal + flux * inverse
                before[q, part, :] = value

    @pl.when(step == rows)
    def _():
        for start, size in chunks:
            part = pl.ds(start, size)
            north = jnp.where(edges_ref[1] > 0, north_ref[part, :], 0.0)
            north_up = face * jnp.maximum(north, 0.0)
            north_down = face * jnp.minimum(north, 0.0)
            for q in range(tracers):
                below = jnp.where(edges_ref[1] > 0, next_ref[q, part, :], 0.0)
                flux = north_up * before[q, part, :] + north_down * below
                out_ref[q, 0, part, :] = partial[q, part, :] - flux * inverse_before


def advect(edges, face, inverse, tracers, courants, filtered, halos):
    count, rows, width, lev = tracers.shape
    fields = filtered.shape[0]

    def clipped(j):
        return (0, jnp.minimum(j, rows - 1), 0, 0)

    smem = pl.BlockSpec(memory_space=pltpu.SMEM)
    vmem = pl.BlockSpec(memory_space=pltpu.VMEM)
    return pl.pallas_call(
        advect_kernel,
        grid=(rows + 1,),
        in_specs=[
            smem,
            smem,
            smem,
            pl.BlockSpec((count, 1, width, lev), clipped),
            pl.BlockSpec((2, 1, width, lev), clipped),
            pl.BlockSpec((fields, 1, width, lev), clipped),
        ]
        + [vmem] * len(halos),
        out_specs=[
            pl.BlockSpec((count, 1, width, lev), lambda j: (0, jnp.maximum(j - 1, 0), 0, 0)),
            pl.BlockSpec((fields, 1, width, lev), clipped),
        ],
        out_shape=[
            jax.ShapeDtypeStruct(tracers.shape, jnp.float32),
            jax.ShapeDtypeStruct(filtered.shape, filtered.dtype),
        ],
        scratch_shapes=[
            pltpu.VMEM((count, width, lev), jnp.float32),
            pltpu.VMEM((count, width, lev), jnp.float32),
            pltpu.VMEM((count, CHUNK + 16, lev), jnp.float32),
            pltpu.VMEM((width + 8, lev), jnp.float32),
        ],
        compiler_params=pltpu.CompilerParams(vmem_limit_bytes=VMEM_BYTES),
        cost_estimate=pl.CostEstimate(
            flops=20 * tracers.size, bytes_accessed=8 * tracers.size, transcendentals=0
        ),
        name="advect_rows",
    )(edges, face, inverse, tracers, courants, filtered, *halos)


def per_device(tendencies, bands, winds, tracers):
    lat_rows, width = tendencies.shape[1:3]
    lat_devices, lon_devices = lax.axis_size("lat"), lax.axis_size("lon")
    lat_count, lon_count = lat_devices * lat_rows, lon_devices * width
    place = lax.axis_index("lat")
    group = 2 - lat_rows % 2

    own_ids = place * lat_rows + jnp.arange(lat_rows, dtype=jnp.int32)
    damping = 0.25 + 0.5 * (own_ids.astype(jnp.float32) + 0.5) / (lat_count / 2.0)
    keep = jnp.where(own_ids < lat_count // 2, damping, 1.0)
    near, far, send, spans = filter_tables(
        2 * jnp.take(bands, own_ids) + 1, 1.0 - keep, lon_count, width, group
    )
    filtered, courants, *halos = filter_rows(
        keep, tendencies, send, near, far, winds, tracers, spans, group
    )
    centre_cos, _ = latitude_factors(own_ids, lat_count)
    _, face_cos = latitude_factors(
        place * lat_rows + jnp.arange(lat_rows + 1, dtype=jnp.int32), lat_count
    )
    edges = jnp.stack([place > 0, place < lat_devices - 1]).astype(jnp.int32)
    advected, filtered = advect(
        edges, face_cos, 1.0 / centre_cos, tracers, courants, filtered, halos
    )
    return (filtered, advected)


def solution(mesh):
    spec = P(None, "lat", "lon", None)
    return jax.shard_map(
        per_device,
        mesh=mesh,
        in_specs=(spec, P(), spec, spec),
        out_specs=(spec, spec),
        check_vma=False,
    )
```

```python
import functools
import math

import jax
import jax.numpy as jnp
import numpy as np
from jax import lax
from jax.experimental import pallas as pl
from jax.experimental.pallas import tpu as pltpu
from jax.sharding import PartitionSpec as P

HEMI = 720
CHUNK = 24
VMEM_BYTES = 56 * 1024 * 1024
FACTOR_FLOOR = 1e-7


def latitude_factors(lat_count):
    row = np.arange(lat_count + 1, dtype=np.float64)
    grid_row = row + (HEMI // 2 - lat_count // 2)
    inverse = 1.0 / np.sin(np.pi * (grid_row[:-1] + 0.5) / (2.0 * HEMI))
    face_cos = np.sin(np.pi * grid_row / (2.0 * HEMI))
    damping = 0.25 + 0.5 * (row[:-1] + 0.5) / (lat_count / 2.0)
    keep = np.where(row[:-1] < lat_count // 2, damping, 1.0)
    return [table.astype(np.float32) for table in (face_cos, inverse, keep)]


@functools.lru_cache(maxsize=None)
def cosecant_factors(lon_count, width, group):
    cells = np.arange(width)
    apart = cells[:, None] - cells[None, :]
    safe = np.where(apart == 0, 1, apart)
    own = np.where(apart == 0, 0.0, 1.0 / (lon_count * np.sin(np.pi * safe / lon_count)))
    step = 8 // group
    targets, sources, part, member, spans = [], [], [], [], []
    start = 0
    for shift in range(1, lon_count // width):
        block = 1.0 / (lon_count * np.sin(np.pi * (apart + shift * width) / lon_count))
        left, values, right = np.linalg.svd(block)
        rank = max(step, -(-int((values > FACTOR_FLOOR).sum()) // step) * step)
        root = np.sqrt(values[:rank])
        targets.append(np.tile(left[:, :rank] * root, (1, 2 * group)))
        sources.append(np.tile(root[:, None] * right[:rank], (2 * group, 1)))
        part.append(np.tile(np.repeat([0, 1], rank), group))
        member.append(np.repeat(np.arange(group), 2 * rank))
        spans.append((shift, start, 2 * group * rank))
        start += 2 * group * rank
    masks = np.stack(
        [
            (np.concatenate(member) == g) & (np.concatenate(part) == which)
            for g in range(group)
            for which in (0, 1)
        ]
    )
    return (
        own.astype(np.float32),
        (np.concatenate(targets, 1) * masks[:, None, :]).astype(np.float32),
        (np.concatenate(sources, 0) * masks[:, :, None]).astype(np.float32),
        tuple(spans),
    )


def waves(odd, cells, lon_count):
    phase = (odd[:, None] * cells[None, :] % (2 * lon_count)).astype(jnp.float32) * (
        math.pi / lon_count
    )
    return jnp.sin(phase), jnp.cos(phase)


def filter_kernel(
    spans, group, halves, keep_ref, own_ref, sin_shift, cos_shift, x_ref, sin_row, cos_row,
    sin_column, cos_column, csc_ref, target_ref, source_ref, winds_ref, tracers_ref,
    filtered_ref, courant_ref, prior_ref, next_ref, west_ref, east_ref, north_ref, zonal_ref,
    winds, filtered, courants, total, outgoing, incoming, low_block, high_block, low, high, column,
    local_sem, send_sem, recv_sem, halo_send, halo_recv,
):
    fields, rows, width, lev = x_ref.shape
    tracer_count = tracers_ref.shape[0]
    lat, lon = lax.axis_index("lat"), lax.axis_index("lon")
    lat_devices, lon_devices = lax.axis_size("lat"), lax.axis_size("lon")
    has_prior, has_next = lat > 0, lat < lat_devices - 1
    lat_prior, lat_next = jnp.maximum(lat - 1, 0), jnp.minimum(lat + 1, lat_devices - 1)
    lon_west, lon_east = lax.rem(lon + lon_devices - 1, lon_devices), lax.rem(lon + 1, lon_devices)
    last_start = (width - 1) // 8 * 8

    winds_copy = pltpu.make_async_copy(winds_ref, winds, local_sem.at[0])
    low_copy = pltpu.make_async_copy(tracers_ref.at[:, :, pl.ds(0, 8)], low_block, local_sem.at[1])
    high_copy = pltpu.make_async_copy(
        tracers_ref.at[:, :, pl.ds(last_start, width - last_start)], high_block, local_sem.at[2]
    )
    low_copy.start()
    high_copy.start()
    winds_copy.start()

    barrier = pltpu.get_barrier_semaphore()
    for shift in range(1, lon_devices):
        pl.semaphore_signal(
            barrier, inc=1, device_id=(lat, lax.rem(lon + shift, lon_devices)),
            device_id_type=pl.DeviceIdType.MESH,
        )

    @pl.when(has_prior)
    def _():
        pl.semaphore_signal(
            barrier, inc=1, device_id=(lat_prior, lon), device_id_type=pl.DeviceIdType.MESH
        )

    @pl.when(has_next)
    def _():
        pl.semaphore_signal(
            barrier, inc=1, device_id=(lat_next, lon), device_id_type=pl.DeviceIdType.MESH
        )

    def field_row(j):
        return jnp.concatenate([x_ref[f, j] for f in range(fields)], axis=1)

    def project(p, carry):
        parts = []
        for g in range(group):
            j = p * group + g
            sines, cosines = sin_row[pl.ds(j, 1), :], cos_row[pl.ds(j, 1), :]
            pieces = []
            for slot, (_, start, size) in enumerate(spans):
                sin_s, cos_s = sin_shift[j, slot], cos_shift[j, slot]
                moved_cos = cosines * cos_s + sines * sin_s
                moved_sin = sines * cos_s - cosines * sin_s
                piece = slice(start, start + size)
                pieces.append(
                    source_ref[2 * g, piece, :] * moved_cos + source_ref[2 * g + 1, piece, :] * moved_sin
                )
            table = jnp.concatenate(pieces, axis=0).astype(jnp.bfloat16)
            parts.append(jnp.dot(table, field_row(j), preferred_element_type=jnp.float32))
        outgoing[p] = sum(parts[1:], parts[0]).astype(jnp.bfloat16)
        return carry

    groups = rows // group // halves
    lax.fori_loop(0, groups, project, 0)
    pl.semaphore_wait(barrier, lon_devices - 1 + has_prior.astype(jnp.int32) + has_next.astype(jnp.int32))

    def remote(source, target, sems, slot, device):
        return pltpu.make_async_remote_copy(
            src_ref=source, dst_ref=target, send_sem=sems[0].at[slot], recv_sem=sems[1].at[slot],
            device_id=device, device_id_type=pl.DeviceIdType.MESH,
        )

    exchanges = [[] for _ in range(halves)]
    for half in range(halves):
        for slot, (shift, start, size) in enumerate(spans):
            part = (pl.ds(half * groups, groups), pl.ds(start, size))
            exchanges[half].append(
                remote(
                    outgoing.at[part], incoming.at[part], (send_sem, recv_sem),
                    half * len(spans) + slot, (lat, lax.rem(lon + shift, lon_devices)),
                )
            )
    for half in range(halves):
        if half > 0:
            lax.fori_loop(half * groups, (half + 1) * groups, project, 0)
        for exchange in exchanges[half]:
            exchange.start()

    halo = (halo_send, halo_recv)
    to_next = remote(tracers_ref.at[:, rows - 1], prior_ref, halo, 0, (lat_next, lon))
    to_prior = remote(tracers_ref.at[:, 0], next_ref, halo, 1, (lat_prior, lon))
    to_east = remote(high, west_ref, halo, 2, (lat, lon_east))
    to_west = remote(low, east_ref, halo, 3, (lat, lon_west))
    north_to_prior = remote(courants.at[1, 0], north_ref, halo, 4, (lat_prior, lon))
    zonal_to_west = remote(column, zonal_ref, halo, 5, (lat, lon_west))

    @pl.when(has_next)
    def _():
        to_next.start()

    @pl.when(has_prior)
    def _():
        to_prior.start()

    low_copy.wait()
    high_copy.wait()
    for q in range(tracer_count):
        for j in range(rows):
            low[q, j : j + 1, :] = low_block[q, j, 0:1, :]
            high[q, j : j + 1, :] = high_block[q, j, width - 1 - last_start : width - last_start, :]
    to_east.start()
    to_west.start()

    def column_of(ref, j):
        return pltpu.roll(ref[...], lax.rem(128 - j, 128), 1)[:, 0:1]

    def near_row(j, carry):
        sines, cosines = sin_row[pl.ds(j, 1), :], cos_row[pl.ds(j, 1), :]
        own_sin, own_cos = column_of(sin_column, j), column_of(cos_column, j)
        table = (own_sin * cosines - own_cos * sines) * csc_ref[...]
        total[j] = jnp.dot(table.astype(jnp.bfloat16), field_row(j), preferred_element_type=jnp.float32)
        return carry

    lax.fori_loop(0, rows, near_row, 0)
    winds_copy.wait()

    def outputs(j):
        return (
            pltpu.make_async_copy(filtered.at[:, j], filtered_ref.at[:, j], local_sem.at[3]),
            pltpu.make_async_copy(courants.at[:, j], courant_ref.at[:, j], local_sem.at[4]),
        )

    def finish(p, g):
        j = p * group + g
        own_sin, own_cos = column_of(sin_column, j), column_of(cos_column, j)
        table = own_sin * target_ref[2 * g] - own_cos * target_ref[2 * g + 1]
        far = jnp.dot(table.astype(jnp.bfloat16), incoming[p], preferred_element_type=jnp.float32)
        keep = keep_ref[lat * rows + j] + own_ref[j]
        for f in range(fields):
            lanes = slice(f * lev, (f + 1) * lev)
            value = keep * x_ref[f, j].astype(jnp.float32) + total[j, :, lanes] + far[:, lanes]
            value = value.astype(jnp.bfloat16)
            filtered[f, j] = value
            if f < 2:
                courant = (0.5 if f == 0 else 0.25) * jnp.tanh(winds[f, j] + value.astype(jnp.float32))
                courants[f, j] = courant
                if f == 0:
                    column[pl.ds(j, 1), :] = courant[0:1, :]
        for copy in outputs(j):
            copy.start()

    def later(p, carry):
        for g in range(group):
            finish(p, g)
        return carry

    for half in range(halves):
        for exchange in exchanges[half]:
            exchange.wait_recv()
        first = half * groups
        if half == 0:
            later(0, 0)

            @pl.when(has_prior)
            def _():
                north_to_prior.start()

            first = 1
        lax.fori_loop(first, (half + 1) * groups, later, 0)
    zonal_to_west.start()

    for exchange in sum(exchanges, []):
        exchange.wait_send()
    to_east.wait()
    to_west.wait()
    zonal_to_west.wait()

    @pl.when(has_next)
    def _():
        to_next.wait_send()
        to_prior.wait_recv()
        north_to_prior.wait_recv()

    @pl.when(has_prior)
    def _():
        to_next.wait_recv()
        to_prior.wait_send()
        north_to_prior.wait_send()

    pltpu.make_async_copy(filtered, filtered_ref, local_sem.at[3]).wait()
    pltpu.make_async_copy(courants, courant_ref, local_sem.at[4]).wait()


def filter_rows(scalars, tendencies, tables, winds, tracers, spans, group):
    fields, rows, width, lev = tendencies.shape
    count = tables[-1].shape[1]
    halves = 2 - rows // group % 2
    tracer_count = tracers.shape[0]
    last = width - (width - 1) // 8 * 8
    hbm = pl.BlockSpec(memory_space=pl.ANY)
    vmem = pl.BlockSpec(memory_space=pltpu.VMEM)
    f32 = jnp.float32
    exchanged = (rows // group, count, fields * lev)
    return pl.pallas_call(
        functools.partial(filter_kernel, spans, group, halves),
        in_specs=[pl.BlockSpec(memory_space=pltpu.SMEM)] * len(scalars)
        + [vmem] * (1 + len(tables))
        + [hbm, hbm],
        out_specs=[hbm] * 8,
        out_shape=[
            jax.ShapeDtypeStruct(tendencies.shape, jnp.bfloat16),
            jax.ShapeDtypeStruct(winds.shape, f32),
            jax.ShapeDtypeStruct((tracer_count, width, lev), f32),
            jax.ShapeDtypeStruct((tracer_count, width, lev), f32),
            jax.ShapeDtypeStruct((tracer_count, rows, lev), f32),
            jax.ShapeDtypeStruct((tracer_count, rows, lev), f32),
            jax.ShapeDtypeStruct((width, lev), f32),
            jax.ShapeDtypeStruct((rows, lev), f32),
        ],
        scratch_shapes=[
            pltpu.VMEM(winds.shape, f32),
            pltpu.VMEM(tendencies.shape, jnp.bfloat16),
            pltpu.VMEM(winds.shape, f32),
            pltpu.VMEM((rows, width, fields * lev), f32),
            pltpu.VMEM(exchanged, jnp.bfloat16),
            pltpu.VMEM(exchanged, jnp.bfloat16),
            pltpu.VMEM((tracer_count, rows, 8, lev), f32),
            pltpu.VMEM((tracer_count, rows, last, lev), f32),
            pltpu.VMEM((tracer_count, rows, lev), f32),
            pltpu.VMEM((tracer_count, rows, lev), f32),
            pltpu.VMEM((rows, lev), f32),
            pltpu.SemaphoreType.DMA((5,)),
            pltpu.SemaphoreType.DMA((halves * len(spans),)),
            pltpu.SemaphoreType.DMA((halves * len(spans),)),
            pltpu.SemaphoreType.DMA((6,)),
            pltpu.SemaphoreType.DMA((6,)),
        ],
        compiler_params=pltpu.CompilerParams(
            vmem_limit_bytes=VMEM_BYTES, collective_id=0, has_side_effects=True
        ),
        cost_estimate=pl.CostEstimate(
            flops=2 * rows * (width + 2 * count) * width * fields * lev,
            bytes_accessed=4 * tendencies.size + 8 * winds.size,
            transcendentals=winds.size,
        ),
        name="filter_rows",
    )(*scalars, tendencies, *tables, winds, tracers)


def advect_kernel(
    face_ref, inverse_ref, tracer_ref, courant_ref, passing_ref, prior_ref, next_ref,
    west_ref, east_ref, north_ref, zonal_ref, out_ref, passed_ref, before, partial, edge, shifted,
):
    tracers, _, width, _ = tracer_ref.shape
    step = pl.program_id(0)
    rows = pl.num_programs(0) - 1
    lat = lax.axis_index("lat")
    has_prior, has_next = lat > 0, lat < lax.axis_size("lat") - 1
    face = face_ref[lat * rows + step]
    inverse_before = inverse_ref[lat * rows + jnp.maximum(step - 1, 0)]
    chunks = [(start, min(CHUNK, width - start)) for start in range(0, width, CHUNK)]

    @pl.when(step == 0)
    def _():
        before[...] = jnp.where(has_prior, prior_ref[...], 0.0)
        partial[...] = jnp.zeros_like(partial)

    @pl.when(step < rows)
    def _():
        inverse = inverse_ref[lat * rows + step]
        passed_ref[...] = passing_ref[...]
        shifted[0:width, :] = courant_ref[0, 0]
        shifted[width : width + 1, :] = zonal_ref[pl.ds(step, 1), :]
        for start, size in chunks:
            part = pl.ds(start, size)
            here = courant_ref[0, 0, part, :]
            there = shifted[pl.ds(start + 1, size), :]
            north = courant_ref[1, 0, part, :]
            here_up, here_down = jnp.maximum(here, 0.0), jnp.minimum(here, 0.0)
            there_up, there_down = jnp.maximum(there, 0.0), jnp.minimum(there, 0.0)
            north_up = face * jnp.maximum(north, 0.0)
            north_down = face * jnp.minimum(north, 0.0)
            for q in range(tracers):
                value = tracer_ref[q, 0, part, :]
                if start == 0:
                    edge[q, 7:8, :] = west_ref[q, pl.ds(step, 1), :]
                    edge[q, pl.ds(8, size), :] = value
                    west = edge[q, pl.ds(7, size), :]
                else:
                    west = tracer_ref[q, 0, pl.ds(start - 1, size), :]
                if start + size == width:
                    edge[q, pl.ds(8, size), :] = value
                    edge[q, pl.ds(8 + size, 1), :] = east_ref[q, pl.ds(step, 1), :]
                    east = edge[q, pl.ds(9, size), :]
                else:
                    east = tracer_ref[q, 0, pl.ds(start + 1, size), :]
                flux = north_up * before[q, part, :] + north_down * value
                out_ref[q, 0, part, :] = partial[q, part, :] - flux * inverse_before
                zonal = (there_up * value + there_down * east) - (here_up * west + here_down * value)
                partial[q, part, :] = value - zonal + flux * inverse
                before[q, part, :] = value

    @pl.when(step == rows)
    def _():
        for start, size in chunks:
            part = pl.ds(start, size)
            north = jnp.where(has_next, north_ref[part, :], 0.0)
            north_up = face * jnp.maximum(north, 0.0)
            north_down = face * jnp.minimum(north, 0.0)
            for q in range(tracers):
                below = jnp.where(has_next, next_ref[q, part, :], 0.0)
                flux = north_up * before[q, part, :] + north_down * below
                out_ref[q, 0, part, :] = partial[q, part, :] - flux * inverse_before


def advect(face, inverse, tracers, courants, filtered, halos):
    count, rows, width, lev = tracers.shape
    fields = filtered.shape[0]

    def clipped(j):
        return (0, jnp.minimum(j, rows - 1), 0, 0)

    smem = pl.BlockSpec(memory_space=pltpu.SMEM)
    vmem = pl.BlockSpec(memory_space=pltpu.VMEM)
    return pl.pallas_call(
        advect_kernel,
        grid=(rows + 1,),
        in_specs=[
            smem,
            smem,
            pl.BlockSpec((count, 1, width, lev), clipped),
            pl.BlockSpec((2, 1, width, lev), clipped),
            pl.BlockSpec((fields, 1, width, lev), clipped),
        ]
        + [vmem] * len(halos),
        out_specs=[
            pl.BlockSpec((count, 1, width, lev), lambda j: (0, jnp.maximum(j - 1, 0), 0, 0)),
            pl.BlockSpec((fields, 1, width, lev), clipped),
        ],
        out_shape=[
            jax.ShapeDtypeStruct(tracers.shape, jnp.float32),
            jax.ShapeDtypeStruct(filtered.shape, filtered.dtype),
        ],
        scratch_shapes=[
            pltpu.VMEM((count, width, lev), jnp.float32),
            pltpu.VMEM((count, width, lev), jnp.float32),
            pltpu.VMEM((count, CHUNK + 16, lev), jnp.float32),
            pltpu.VMEM((width + 8, lev), jnp.float32),
        ],
        compiler_params=pltpu.CompilerParams(vmem_limit_bytes=VMEM_BYTES),
        cost_estimate=pl.CostEstimate(
            flops=20 * tracers.size, bytes_accessed=8 * tracers.size, transcendentals=0
        ),
        name="advect_rows",
    )(face, inverse, tracers, courants, filtered, *halos)


def per_device(tendencies, bands, winds, tracers):
    lat_rows, width = tendencies.shape[1:3]
    lat_devices, lon_devices = lax.axis_size("lat"), lax.axis_size("lon")
    lat_count, lon_count = lat_devices * lat_rows, lon_devices * width
    place = lax.axis_index("lat")
    group = 2 - lat_rows % 2

    face_cos, inverse, keep = latitude_factors(lat_count)
    csc, targets, sources, spans = cosecant_factors(lon_count, width, group)
    odd = 2 * lax.dynamic_slice_in_dim(bands, place * lat_rows, lat_rows) + 1
    strength = 1.0 - lax.dynamic_slice_in_dim(jnp.asarray(keep), place * lat_rows, lat_rows)
    sin_row, cos_row = waves(odd, jnp.arange(width, dtype=jnp.int32), lon_count)
    shifts = np.array([shift * width for shift, _, _ in spans], np.int32)
    sin_shift, cos_shift = waves(odd, jnp.asarray(shifts), lon_count)
    columns = [
        jnp.pad((table * strength[:, None]).T, ((0, 0), (0, 128 - lat_rows)))
        for table in (sin_row, cos_row)
    ]
    own = strength * odd.astype(jnp.float32) / lon_count
    filtered, courants, *halos = filter_rows(
        (jnp.asarray(keep), own, sin_shift, cos_shift),
        tendencies,
        (sin_row, cos_row, *columns, jnp.asarray(csc), jnp.asarray(targets), jnp.asarray(sources)),
        winds, tracers, spans, group,
    )
    advected, filtered = advect(
        jnp.asarray(face_cos), jnp.asarray(inverse), tracers, courants, filtered, halos
    )
    return (filtered, advected)


def solution(mesh):
    spec = P(None, "lat", "lon", None)
    return jax.shard_map(
        per_device,
        mesh=mesh,
        in_specs=(spec, P(), spec, spec),
        out_specs=(spec, spec),
        check_vma=False,
    )
```

```python
import functools
import math

import jax
import jax.numpy as jnp
import numpy as np
from jax import lax
from jax.experimental import pallas as pl
from jax.experimental.pallas import tpu as pltpu
from jax.sharding import PartitionSpec as P

HEMI = 720
CHUNK = 24
VMEM_BYTES = 56 * 1024 * 1024
FACTOR_FLOOR = 1e-7


def latitude_factors(lat_count):
    row = np.arange(lat_count + 1, dtype=np.float64)
    grid_row = row + (HEMI // 2 - lat_count // 2)
    inverse = 1.0 / np.sin(np.pi * (grid_row[:-1] + 0.5) / (2.0 * HEMI))
    face_cos = np.sin(np.pi * grid_row / (2.0 * HEMI))
    damping = 0.25 + 0.5 * (row[:-1] + 0.5) / (lat_count / 2.0)
    keep = np.where(row[:-1] < lat_count // 2, damping, 1.0)
    return [table.astype(np.float32) for table in (face_cos, inverse, keep)]


@functools.lru_cache(maxsize=None)
def cosecant_factors(lon_count, width, group):
    cells = np.arange(width)
    apart = cells[:, None] - cells[None, :]
    safe = np.where(apart == 0, 1, apart)
    own = np.where(apart == 0, 0.0, 1.0 / (lon_count * np.sin(np.pi * safe / lon_count)))
    step = 8 // group
    targets, sources, part, member, spans = [], [], [], [], []
    start = 0
    for shift in range(1, lon_count // width):
        block = 1.0 / (lon_count * np.sin(np.pi * (apart + shift * width) / lon_count))
        left, values, right = np.linalg.svd(block)
        rank = max(step, -(-int((values > FACTOR_FLOOR).sum()) // step) * step)
        root = np.sqrt(values[:rank])
        targets.append(np.tile(left[:, :rank] * root, (1, 2 * group)))
        sources.append(np.tile(root[:, None] * right[:rank], (2 * group, 1)))
        part.append(np.tile(np.repeat([0, 1], rank), group))
        member.append(np.repeat(np.arange(group), 2 * rank))
        spans.append((shift, start, 2 * group * rank))
        start += 2 * group * rank
    masks = np.stack(
        [
            (np.concatenate(member) == g) & (np.concatenate(part) == which)
            for g in range(group)
            for which in (0, 1)
        ]
    )
    return (
        own.astype(np.float32),
        (np.concatenate(targets, 1) * masks[:, None, :]).astype(np.float32),
        (np.concatenate(sources, 0) * masks[:, :, None]).astype(np.float32),
        tuple(spans),
    )


def waves(odd, cells, lon_count):
    phase = (odd[:, None] * cells[None, :] % (2 * lon_count)).astype(jnp.float32) * (
        math.pi / lon_count
    )
    return jnp.sin(phase), jnp.cos(phase)


def filter_kernel(
    spans, group, halves, keep_ref, own_ref, sin_shift, cos_shift, x_ref, sin_row, cos_row,
    sin_column, cos_column, csc_ref, target_ref, source_ref, winds_ref, tracers_ref,
    filtered_ref, courant_ref, prior_ref, next_ref, west_ref, east_ref, north_ref, zonal_ref,
    winds, filtered, courants, total, outgoing, incoming, low_block, high_block, low, high, column,
    local_sem, send_sem, recv_sem, halo_send, halo_recv,
):
    fields, rows, width, lev = x_ref.shape
    tracer_count = tracers_ref.shape[0]
    lat, lon = lax.axis_index("lat"), lax.axis_index("lon")
    lat_devices, lon_devices = lax.axis_size("lat"), lax.axis_size("lon")
    has_prior, has_next = lat > 0, lat < lat_devices - 1
    lat_prior, lat_next = jnp.maximum(lat - 1, 0), jnp.minimum(lat + 1, lat_devices - 1)
    lon_west, lon_east = lax.rem(lon + lon_devices - 1, lon_devices), lax.rem(lon + 1, lon_devices)
    last_start = (width - 1) // 8 * 8

    winds_copy = pltpu.make_async_copy(winds_ref, winds, local_sem.at[0])
    low_copy = pltpu.make_async_copy(tracers_ref.at[:, :, pl.ds(0, 8)], low_block, local_sem.at[1])
    high_copy = pltpu.make_async_copy(
        tracers_ref.at[:, :, pl.ds(last_start, width - last_start)], high_block, local_sem.at[2]
    )
    low_copy.start()
    high_copy.start()
    winds_copy.start()

    barrier = pltpu.get_barrier_semaphore()
    for shift in range(1, lon_devices):
        pl.semaphore_signal(
            barrier, inc=1, device_id=(lat, lax.rem(lon + shift, lon_devices)),
            device_id_type=pl.DeviceIdType.MESH,
        )

    @pl.when(has_prior)
    def _():
        pl.semaphore_signal(
            barrier, inc=1, device_id=(lat_prior, lon), device_id_type=pl.DeviceIdType.MESH
        )

    @pl.when(has_next)
    def _():
        pl.semaphore_signal(
            barrier, inc=1, device_id=(lat_next, lon), device_id_type=pl.DeviceIdType.MESH
        )

    def field_row(j):
        return jnp.concatenate([x_ref[f, j] for f in range(fields)], axis=1)

    def project(p, carry):
        parts = []
        for g in range(group):
            j = p * group + g
            sines, cosines = sin_row[pl.ds(j, 1), :], cos_row[pl.ds(j, 1), :]
            pieces = []
            for slot, (_, start, size) in enumerate(spans):
                sin_s, cos_s = sin_shift[j, slot], cos_shift[j, slot]
                moved_cos = cosines * cos_s + sines * sin_s
                moved_sin = sines * cos_s - cosines * sin_s
                piece = slice(start, start + size)
                pieces.append(
                    source_ref[2 * g, piece, :] * moved_cos + source_ref[2 * g + 1, piece, :] * moved_sin
                )
            table = jnp.concatenate(pieces, axis=0).astype(jnp.bfloat16)
            parts.append(jnp.dot(table, field_row(j), preferred_element_type=jnp.float32))
        outgoing[p] = sum(parts[1:], parts[0]).astype(jnp.bfloat16)
        return carry

    groups = rows // group // halves
    lax.fori_loop(0, groups, project, 0)
    pl.semaphore_wait(barrier, lon_devices - 1 + has_prior.astype(jnp.int32) + has_next.astype(jnp.int32))

    def remote(source, target, sems, slot, device):
        return pltpu.make_async_remote_copy(
            src_ref=source, dst_ref=target, send_sem=sems[0].at[slot], recv_sem=sems[1].at[slot],
            device_id=device, device_id_type=pl.DeviceIdType.MESH,
        )

    exchanges = [[] for _ in range(halves)]
    for half in range(halves):
        for slot, (shift, start, size) in enumerate(spans):
            part = (pl.ds(half * groups, groups), pl.ds(start, size))
            exchanges[half].append(
                remote(
                    outgoing.at[part], incoming.at[part], (send_sem, recv_sem),
                    half * len(spans) + slot, (lat, lax.rem(lon + shift, lon_devices)),
                )
            )
    for half in range(halves):
        if half > 0:
            lax.fori_loop(half * groups, (half + 1) * groups, project, 0)
        for exchange in exchanges[half]:
            exchange.start()

    halo = (halo_send, halo_recv)
    to_next = remote(tracers_ref.at[:, rows - 1], prior_ref, halo, 0, (lat_next, lon))
    to_prior = remote(tracers_ref.at[:, 0], next_ref, halo, 1, (lat_prior, lon))
    to_east = remote(high, west_ref, halo, 2, (lat, lon_east))
    to_west = remote(low, east_ref, halo, 3, (lat, lon_west))
    north_to_prior = remote(courants.at[1, 0], north_ref, halo, 4, (lat_prior, lon))
    zonal_to_west = remote(column, zonal_ref, halo, 5, (lat, lon_west))

    @pl.when(has_next)
    def _():
        to_next.start()

    @pl.when(has_prior)
    def _():
        to_prior.start()

    low_copy.wait()
    high_copy.wait()
    for q in range(tracer_count):
        for j in range(rows):
            low[q, j : j + 1, :] = low_block[q, j, 0:1, :]
            high[q, j : j + 1, :] = high_block[q, j, width - 1 - last_start : width - last_start, :]
    to_east.start()
    to_west.start()

    def column_of(ref, j):
        return pltpu.roll(ref[...], lax.rem(128 - j, 128), 1)[:, 0:1]

    def near_row(j, carry):
        sines, cosines = sin_row[pl.ds(j, 1), :], cos_row[pl.ds(j, 1), :]
        own_sin, own_cos = column_of(sin_column, j), column_of(cos_column, j)
        table = (own_sin * cosines - own_cos * sines) * csc_ref[...]
        total[j] = jnp.dot(table.astype(jnp.bfloat16), field_row(j), preferred_element_type=jnp.float32)
        return carry

    lax.fori_loop(0, rows, near_row, 0)
    winds_copy.wait()

    def outputs(j):
        return (
            pltpu.make_async_copy(filtered.at[:, j], filtered_ref.at[:, j], local_sem.at[3]),
            pltpu.make_async_copy(courants.at[:, j], courant_ref.at[:, j], local_sem.at[4]),
        )

    def finish(p, g):
        j = p * group + g
        own_sin, own_cos = column_of(sin_column, j), column_of(cos_column, j)
        table = own_sin * target_ref[2 * g] - own_cos * target_ref[2 * g + 1]
        far = jnp.dot(table.astype(jnp.bfloat16), incoming[p], preferred_element_type=jnp.float32)
        keep = keep_ref[lat * rows + j] + own_ref[j]
        for f in range(fields):
            lanes = slice(f * lev, (f + 1) * lev)
            value = keep * x_ref[f, j].astype(jnp.float32) + total[j, :, lanes] + far[:, lanes]
            value = value.astype(jnp.bfloat16)
            filtered[f, j] = value
            if f < 2:
                courant = (0.5 if f == 0 else 0.25) * jnp.tanh(winds[f, j] + value.astype(jnp.float32))
                courants[f, j] = courant
                if f == 0:
                    column[pl.ds(j, 1), :] = courant[0:1, :]
        for copy in outputs(j):
            copy.start()

    def later(p, carry):
        for g in range(group):
            finish(p, g)
        return carry

    for half in range(halves):
        for exchange in exchanges[half]:
            exchange.wait_recv()
        first = half * groups
        if half == 0:
            later(0, 0)

            @pl.when(has_prior)
            def _():
                north_to_prior.start()

            first = 1
        lax.fori_loop(first, (half + 1) * groups, later, 0)
    zonal_to_west.start()

    for exchange in sum(exchanges, []):
        exchange.wait_send()
    to_east.wait()
    to_west.wait()
    zonal_to_west.wait()

    @pl.when(has_next)
    def _():
        to_next.wait_send()
        to_prior.wait_recv()
        north_to_prior.wait_recv()

    @pl.when(has_prior)
    def _():
        to_next.wait_recv()
        to_prior.wait_send()
        north_to_prior.wait_send()

    pltpu.make_async_copy(filtered, filtered_ref, local_sem.at[3]).wait()
    pltpu.make_async_copy(courants, courant_ref, local_sem.at[4]).wait()


def filter_rows(scalars, tendencies, tables, winds, tracers, spans, group):
    fields, rows, width, lev = tendencies.shape
    count = tables[-1].shape[1]
    halves = 2 - rows // group % 2
    tracer_count = tracers.shape[0]
    last = width - (width - 1) // 8 * 8
    hbm = pl.BlockSpec(memory_space=pl.ANY)
    vmem = pl.BlockSpec(memory_space=pltpu.VMEM)
    f32 = jnp.float32
    exchanged = (rows // group, count, fields * lev)
    return pl.pallas_call(
        functools.partial(filter_kernel, spans, group, halves),
        in_specs=[pl.BlockSpec(memory_space=pltpu.SMEM)] * len(scalars)
        + [vmem] * (1 + len(tables))
        + [hbm, hbm],
        out_specs=[hbm] * 8,
        out_shape=[
            jax.ShapeDtypeStruct(tendencies.shape, jnp.bfloat16),
            jax.ShapeDtypeStruct(winds.shape, f32),
            jax.ShapeDtypeStruct((tracer_count, width, lev), f32),
            jax.ShapeDtypeStruct((tracer_count, width, lev), f32),
            jax.ShapeDtypeStruct((tracer_count, rows, lev), f32),
            jax.ShapeDtypeStruct((tracer_count, rows, lev), f32),
            jax.ShapeDtypeStruct((width, lev), f32),
            jax.ShapeDtypeStruct((rows, lev), f32),
        ],
        scratch_shapes=[
            pltpu.VMEM(winds.shape, f32),
            pltpu.VMEM(tendencies.shape, jnp.bfloat16),
            pltpu.VMEM(winds.shape, f32),
            pltpu.VMEM((rows, width, fields * lev), f32),
            pltpu.VMEM(exchanged, jnp.bfloat16),
            pltpu.VMEM(exchanged, jnp.bfloat16),
            pltpu.VMEM((tracer_count, rows, 8, lev), f32),
            pltpu.VMEM((tracer_count, rows, last, lev), f32),
            pltpu.VMEM((tracer_count, rows, lev), f32),
            pltpu.VMEM((tracer_count, rows, lev), f32),
            pltpu.VMEM((rows, lev), f32),
            pltpu.SemaphoreType.DMA((5,)),
            pltpu.SemaphoreType.DMA((halves * len(spans),)),
            pltpu.SemaphoreType.DMA((halves * len(spans),)),
            pltpu.SemaphoreType.DMA((6,)),
            pltpu.SemaphoreType.DMA((6,)),
        ],
        compiler_params=pltpu.CompilerParams(
            vmem_limit_bytes=VMEM_BYTES, collective_id=0, has_side_effects=True
        ),
        cost_estimate=pl.CostEstimate(
            flops=2 * rows * (width + 2 * count) * width * fields * lev,
            bytes_accessed=4 * tendencies.size + 8 * winds.size,
            transcendentals=winds.size,
        ),
        name="filter_rows",
    )(*scalars, tendencies, *tables, winds, tracers)


def advect_kernel(
    face_ref, inverse_ref, tracer_ref, courant_ref, passing_ref, prior_ref, next_ref,
    west_ref, east_ref, north_ref, zonal_ref, out_ref, passed_ref, before, partial, edge, shifted,
):
    tracers, _, width, _ = tracer_ref.shape
    step = pl.program_id(0)
    rows = pl.num_programs(0) - 1
    lat = lax.axis_index("lat")
    has_prior, has_next = lat > 0, lat < lax.axis_size("lat") - 1
    face = face_ref[lat * rows + step]
    inverse_before = inverse_ref[lat * rows + jnp.maximum(step - 1, 0)]
    chunks = [(start, min(CHUNK, width - start)) for start in range(0, width, CHUNK)]

    @pl.when(step == 0)
    def _():
        before[...] = jnp.where(has_prior, prior_ref[...], 0.0)
        partial[...] = jnp.zeros_like(partial)

    @pl.when(step < rows)
    def _():
        inverse = inverse_ref[lat * rows + step]
        passed_ref[...] = passing_ref[...]
        shifted[0:width, :] = courant_ref[0, 0]
        shifted[width : width + 1, :] = zonal_ref[pl.ds(step, 1), :]
        for start, size in chunks:
            part = pl.ds(start, size)
            here = courant_ref[0, 0, part, :]
            there = shifted[pl.ds(start + 1, size), :]
            north = courant_ref[1, 0, part, :]
            here_up, here_down = jnp.maximum(here, 0.0), jnp.minimum(here, 0.0)
            there_up, there_down = jnp.maximum(there, 0.0), jnp.minimum(there, 0.0)
            north_up = face * jnp.maximum(north, 0.0)
            north_down = face * jnp.minimum(north, 0.0)
            before_share = north_up * inverse
            value_share = (1.0 - there_up + here_down) + north_down * inverse
            before_taken = north_up * inverse_before
            value_taken = north_down * inverse_before
            for q in range(tracers):
                value = tracer_ref[q, 0, part, :]
                if start == 0:
                    edge[q, 7:8, :] = west_ref[q, pl.ds(step, 1), :]
                    edge[q, pl.ds(8, size), :] = value
                    west = edge[q, pl.ds(7, size), :]
                else:
                    west = tracer_ref[q, 0, pl.ds(start - 1, size), :]
                if start + size == width:
                    edge[q, pl.ds(8, size), :] = value
                    edge[q, pl.ds(8 + size, 1), :] = east_ref[q, pl.ds(step, 1), :]
                    east = edge[q, pl.ds(9, size), :]
                else:
                    east = tracer_ref[q, 0, pl.ds(start + 1, size), :]
                prior = before[q, part, :]
                out_ref[q, 0, part, :] = partial[q, part, :] - before_taken * prior - value_taken * value
                partial[q, part, :] = (
                    value_share * value + before_share * prior + here_up * west - there_down * east
                )
                before[q, part, :] = value

    @pl.when(step == rows)
    def _():
        for start, size in chunks:
            part = pl.ds(start, size)
            north = jnp.where(has_next, north_ref[part, :], 0.0)
            north_up = face * jnp.maximum(north, 0.0)
            north_down = face * jnp.minimum(north, 0.0)
            for q in range(tracers):
                below = jnp.where(has_next, next_ref[q, part, :], 0.0)
                flux = north_up * before[q, part, :] + north_down * below
                out_ref[q, 0, part, :] = partial[q, part, :] - flux * inverse_before


def advect(face, inverse, tracers, courants, filtered, halos):
    count, rows, width, lev = tracers.shape
    fields = filtered.shape[0]

    def clipped(j):
        return (0, jnp.minimum(j, rows - 1), 0, 0)

    smem = pl.BlockSpec(memory_space=pltpu.SMEM)
    vmem = pl.BlockSpec(memory_space=pltpu.VMEM)
    return pl.pallas_call(
        advect_kernel,
        grid=(rows + 1,),
        in_specs=[
            smem,
            smem,
            pl.BlockSpec((count, 1, width, lev), clipped),
            pl.BlockSpec((2, 1, width, lev), clipped),
            pl.BlockSpec((fields, 1, width, lev), clipped),
        ]
        + [vmem] * len(halos),
        out_specs=[
            pl.BlockSpec((count, 1, width, lev), lambda j: (0, jnp.maximum(j - 1, 0), 0, 0)),
            pl.BlockSpec((fields, 1, width, lev), clipped),
        ],
        out_shape=[
            jax.ShapeDtypeStruct(tracers.shape, jnp.float32),
            jax.ShapeDtypeStruct(filtered.shape, filtered.dtype),
        ],
        scratch_shapes=[
            pltpu.VMEM((count, width, lev), jnp.float32),
            pltpu.VMEM((count, width, lev), jnp.float32),
            pltpu.VMEM((count, CHUNK + 16, lev), jnp.float32),
            pltpu.VMEM((width + 8, lev), jnp.float32),
        ],
        compiler_params=pltpu.CompilerParams(vmem_limit_bytes=VMEM_BYTES),
        cost_estimate=pl.CostEstimate(
            flops=20 * tracers.size, bytes_accessed=8 * tracers.size, transcendentals=0
        ),
        name="advect_rows",
    )(face, inverse, tracers, courants, filtered, *halos)


def per_device(tendencies, bands, winds, tracers):
    lat_rows, width = tendencies.shape[1:3]
    lat_devices, lon_devices = lax.axis_size("lat"), lax.axis_size("lon")
    lat_count, lon_count = lat_devices * lat_rows, lon_devices * width
    place = lax.axis_index("lat")
    group = 2 - lat_rows % 2

    face_cos, inverse, keep = latitude_factors(lat_count)
    csc, targets, sources, spans = cosecant_factors(lon_count, width, group)
    odd = 2 * lax.dynamic_slice_in_dim(bands, place * lat_rows, lat_rows) + 1
    strength = 1.0 - lax.dynamic_slice_in_dim(jnp.asarray(keep), place * lat_rows, lat_rows)
    sin_row, cos_row = waves(odd, jnp.arange(width, dtype=jnp.int32), lon_count)
    shifts = np.array([shift * width for shift, _, _ in spans], np.int32)
    sin_shift, cos_shift = waves(odd, jnp.asarray(shifts), lon_count)
    spare = (0, 128 - lat_rows)
    column_phase = (
        jnp.arange(width, dtype=jnp.int32)[:, None] * jnp.pad(odd, spare)[None, :] % (2 * lon_count)
    ).astype(jnp.float32) * (math.pi / lon_count)
    column_scale = jnp.pad(strength, spare)[None, :]
    columns = [jnp.sin(column_phase) * column_scale, jnp.cos(column_phase) * column_scale]
    own = strength * odd.astype(jnp.float32) / lon_count
    filtered, courants, *halos = filter_rows(
        (jnp.asarray(keep), own, sin_shift, cos_shift),
        tendencies,
        (sin_row, cos_row, *columns, jnp.asarray(csc), jnp.asarray(targets), jnp.asarray(sources)),
        winds, tracers, spans, group,
    )
    advected, filtered = advect(
        jnp.asarray(face_cos), jnp.asarray(inverse), tracers, courants, filtered, halos
    )
    return (filtered, advected)


def solution(mesh):
    spec = P(None, "lat", "lon", None)
    return jax.shard_map(
        per_device,
        mesh=mesh,
        in_specs=(spec, P(), spec, spec),
        out_specs=(spec, spec),
        check_vma=False,
    )
```
